128 devices in a mesh: row: 8 (over y, x_lo), col: 16 (over x_hi, z, core).
Axes of the slice: x: 4 (x_hi: 2, x_lo: 2; x = x_hi * 2 + x_lo), y: 4, z: 4, core: 2. Of those that a mesh axis runs over, the one named last changes fastest.
Arguments:
- points: bfloat16 [1048576, 256], P(('row', 'col')), may hold values from -6 to 6
- leaf_bases: bfloat16 [1048576, 128], P(('row', 'col')), may hold values from -0.25 to 0.25
- own_maps: bfloat16 [4, 2048, 128, 128], P(None, ('row', 'col')), may hold values from -0.375 to 0.375
- partner_maps: bfloat16 [4, 2048, 128, 128], P(None, ('row', 'col')), may hold values from -0.375 to 0.375
- expand_bases: bfloat16 [1048576, 128], P(('row', 'col')), may hold values from -0.5 to 0.5
- ranks: int32 [5, 2048], P(None, ('row', 'col')), may hold values from 64 to 128
Outputs:
- scattered: bfloat16 [1048576, 256], P(('row', 'col'))
The draws below stay inside these ranges and needn't reach their ends.
All inputs are finite; a program needn't handle non-finite values.
Results may differ from the reference program's by a relative error of at most 0.009.
Values may be sent and summed in bfloat16 or wider, within the bound.
No kernel may reach another device: no remote copies, remote signals or barrier semaphores. Data moves between devices by JAX's collectives and lax.ppermute only.
A program may use at most 64 MiB of HBM per device.

```python
import math
import jax
import jax.numpy as jnp
from jax import lax

K = 128
R = 256
LEAF = 512
LEVELS = 4
B_DEV = 16
NBLK = 2048
N = 1048576
PIECE = 64
N_ROW = 8
N_COL = 16


def with_ends(array, rng, smallest, largest):
    longest = array.shape.index(max(array.shape))
    spots = []
    for shift in (0, 1):
        where = [jax.random.randint(jax.random.fold_in(rng, axis), (), 0, length) for axis, length in enumerate(array.shape)]
        where[longest] = (where[longest] + shift) % array.shape[longest]
        spots.append(tuple(where))
    return array.at[spots[0]].set(smallest).at[spots[1]].set(largest)


def block_scale(stream_key, extent, shards, least, top_value):
    gain, own = 1.0, jax.random.fold_in(stream_key, 6)
    for dim, blocks in shards:
        steps = jnp.exp(jax.random.uniform(jax.random.fold_in(own, dim), (blocks,), jnp.float32, least / len(shards), top_value / len(shards)))
        gain = gain * jnp.repeat(steps, extent[dim] // blocks).reshape([-1 if axis == dim else 1 for axis in range(len(extent))])
    return gain


def normal_values(key, extent, deviation, reach, pieces=(), kind=jnp.bfloat16):
    values = deviation * jax.random.normal(key, extent, jnp.float32)
    if pieces:
        values = values * block_scale(key, extent, pieces, -0.22, 0.18)
    return jnp.clip(values, -reach, reach).astype(kind)


def setup_inputs(seed: int = 0) -> dict:
    keys = jax.random.split(jax.random.key(seed), 7)
    points = normal_values(keys[0], (N, R), 1.0, 6.0, ((0, 128),))
    leaf_bases = normal_values(keys[1], (N, K), LEAF ** -0.5, 0.25, ((0, 128),))
    own_maps = normal_values(keys[2], (LEVELS, NBLK, K, K), (2 * K) ** -0.5, 0.375, ((1, 128),))
    partner_maps = normal_values(keys[3], (LEVELS, NBLK, K, K), (2 * K) ** -0.5, 0.375, ((1, 128),))
    expand_bases = normal_values(keys[4], (N, K), K ** -0.5, 0.5, ((0, 128),))
    ranks = with_ends(jax.random.randint(keys[5], (LEVELS + 1, NBLK), K // 2, K + 1), jax.random.fold_in(keys[5], 1), K // 2, K).astype(jnp.int32)
    return {"points": points, "leaf_bases": leaf_bases, "own_maps": own_maps, "partner_maps": partner_maps, "expand_bases": expand_bases, "ranks": ranks}


def grouped(fn, arrays):
    count = arrays[0].shape[0]
    size = math.gcd(count, 32)
    shaped = [a.reshape((count // size, size) + a.shape[1:]) for a in arrays]
    result = lax.map(lambda items: fn(*items), tuple(shaped))
    return result.reshape((count,) + result.shape[2:])


def project(bases, values):
    return jnp.einsum('blk,blr->bkr', bases.astype(jnp.float32), values.astype(jnp.float32))


def expand(bases, state):
    return jnp.einsum('blk,bkr->blr', bases.astype(jnp.float32), state.astype(jnp.float32)).astype(jnp.bfloat16)


def combine(own, state, partner, other):
    first = jnp.einsum('bij,bjr->bir', own.astype(jnp.float32), state.astype(jnp.float32))
    second = jnp.einsum('bij,bjr->bir', partner.astype(jnp.float32), other.astype(jnp.float32))
    return first + second


def reference(points, leaf_bases, own_maps, partner_maps, expand_bases, ranks):
    devices = N_ROW * N_COL
    moved = points.reshape(devices, devices, PIECE, R).transpose(1, 0, 2, 3).reshape(NBLK, LEAF, R)
    columns = jnp.arange(K, dtype=jnp.int32)
    keep = (columns[None, None, :] < ranks[:, :, None]).astype(jnp.float32)[..., None]
    coeff = grouped(project, [leaf_bases.reshape(NBLK, LEAF, K), moved])
    state = (coeff * keep[0]).astype(jnp.bfloat16)
    col_bits = N_COL.bit_length() - 1
    row_bits = N_ROW.bit_length() - 1
    flat_bits = [col_bits - 1, col_bits - 2, col_bits - 3, col_bits + row_bits - 1]
    device_ids = jnp.arange(devices, dtype=jnp.int32)
    for level in range(LEVELS):
        partner_ids = device_ids ^ (1 << flat_bits[level])
        other = state.reshape(devices, B_DEV, K, R)[partner_ids].reshape(NBLK, K, R)
        mixed = grouped(combine, [own_maps[level], state, partner_maps[level], other])
        state = (mixed * keep[level + 1]).astype(jnp.bfloat16)
    result = grouped(expand, [expand_bases.reshape(NBLK, LEAF, K), state])
    return result.reshape(N, R)
```

```python
import functools

import jax
import jax.numpy as jnp
from jax import lax
from jax.experimental import pallas as pl
from jax.experimental.pallas import tpu as pltpu
from jax.sharding import PartitionSpec as P

LEAF = 512
SIZES = [4, 4, 4, 4]
VMEM = pl.BlockSpec(memory_space=pltpu.VMEM)
ANY = pl.BlockSpec(memory_space=pl.ANY)


def swapped(block, axis, apart):
    count = lax.axis_size(axis)
    return lax.ppermute(block, axis, [(i, i ^ (1 << apart)) for i in range(count)])


def leaf_kernel(first, moved, bases, out, held, arrived):
    count = out.shape[0]
    copies = []
    for i in range(count):
        copy = pltpu.make_async_copy(moved.at[pl.ds((first + i) * LEAF, LEAF)], held.at[i], arrived.at[i])
        copy.start()
        copies.append(copy)
    for i in range(count):
        copies[i].wait()
        out[i] = jnp.dot(bases[first + i], held[i], preferred_element_type=jnp.float32).astype(jnp.bfloat16)


def mixed(maps, state, other):
    values = jnp.concatenate([state, other], axis=0)
    return jnp.dot(maps, values, preferred_element_type=jnp.float32).astype(jnp.bfloat16)


def level_kernel(level, first, maps, state, other, out):
    for i in range(state.shape[0]):
        out[i] = mixed(maps[level - 1, first + i], state[i], other[i])


def last_kernel(level, first, maps, state, other, expand, *rest):
    out, held, sent = rest[-3:]
    copies = []
    for i in range(state.shape[0]):
        g = first + i
        final = mixed(maps[level - 1, g], state[i], other[i])
        rows = expand[pl.ds(g * LEAF, LEAF), :]
        held[i] = jnp.dot(rows, final, preferred_element_type=jnp.float32).astype(jnp.bfloat16)
        copy = pltpu.make_async_copy(held.at[i], out.at[pl.ds(g * LEAF, LEAF)], sent.at[i])
        copy.start()
        copies.append(copy)
    for copy in copies:
        copy.wait()


def limit(mib):
    return pltpu.CompilerParams(vmem_limit_bytes=mib * 1024 * 1024)


def cost(flops, size):
    return pl.CostEstimate(flops=flops, bytes_accessed=size, transcendentals=0)


def project(moved, bases, first, count):
    rhs, rank_max = moved.shape[1], bases.shape[1]
    return pl.pallas_call(
        functools.partial(leaf_kernel, first),
        out_shape=jax.ShapeDtypeStruct((count, rank_max, rhs), jnp.bfloat16),
        in_specs=[ANY, VMEM],
        out_specs=VMEM,
        scratch_shapes=[pltpu.VMEM((count, LEAF, rhs), jnp.bfloat16), pltpu.SemaphoreType.DMA((count,))],
        compiler_params=limit(24),
        cost_estimate=cost(2 * count * LEAF * rank_max * rhs, count * LEAF * rhs * 2),
        name="leaf",
    )(moved, bases)


def advance(state, other, maps, level, first):
    count, rank_max, rhs = state.shape
    return pl.pallas_call(
        functools.partial(level_kernel, level, first),
        out_shape=jax.ShapeDtypeStruct(state.shape, jnp.bfloat16),
        in_specs=[VMEM] * 3,
        out_specs=VMEM,
        compiler_params=limit(24),
        cost_estimate=cost(4 * count * rank_max * rank_max * rhs, count * rank_max * rhs * 2),
        name="level",
    )(maps, state, other)


def finish(state, other, maps, expand, level, first, so_far):
    count, rank_max, rhs = state.shape
    args = [maps, state, other, expand]
    specs = [VMEM] * 4
    alias = {}
    if so_far is not None:
        alias = {len(args): 0}
        args.append(so_far)
        specs.append(ANY)
    return pl.pallas_call(
        functools.partial(last_kernel, level, first),
        out_shape=jax.ShapeDtypeStruct((expand.shape[0], rhs), jnp.bfloat16),
        in_specs=specs,
        out_specs=ANY,
        scratch_shapes=[pltpu.VMEM((count, LEAF, rhs), jnp.bfloat16), pltpu.SemaphoreType.DMA((count,))],
        input_output_aliases=alias,
        compiler_params=limit(24),
        cost_estimate=cost(2 * count * rank_max * rhs * (LEAF + 2 * rank_max), count * LEAF * rhs * 2),
        name="finish",
    )(*args)


def on_device(points, leaf_bases, own_maps, partner_maps, expand_bases, ranks):
    moved = lax.all_to_all(points, ("row", "col"), split_axis=0, concat_axis=0, tiled=True)
    rank_max = leaf_bases.shape[1]
    keep = (jnp.arange(rank_max, dtype=jnp.int32) < ranks[:, :, None])[..., None]
    bases = jnp.where(keep[0], leaf_bases.reshape(-1, LEAF, rank_max).transpose(0, 2, 1), 0)
    maps = jnp.where(keep[1:], jnp.concatenate([own_maps, partner_maps], axis=3), 0)
    moved, bases, maps = lax.optimization_barrier((moved, bases, maps))
    col_bits = lax.axis_size("col").bit_length() - 1
    row_bits = lax.axis_size("row").bit_length() - 1
    pairs = [("col", col_bits - 1), ("col", col_bits - 2), ("col", col_bits - 3), ("row", row_bits - 1)]
    firsts = [sum(SIZES[:c]) for c in range(len(SIZES))]
    states = [project(moved, bases, f, n) for f, n in zip(firsts, SIZES)]
    for level in range(1, 4):
        others = [swapped(s, *pairs[level - 1]) for s in states]
        states = [advance(s, o, maps, level, f) for f, s, o in zip(firsts, states, others)]
    others = [swapped(s, *pairs[3]) for s in states]
    result = None
    for f, s, o in zip(firsts, states, others):
        result = finish(s, o, maps, expand_bases, 4, f, result)
    return result


def solution(mesh):
    return jax.shard_map(
        on_device,
        mesh=mesh,
        in_specs=(
            P(("row", "col"), None),
            P(("row", "col"), None),
            P(None, ("row", "col"), None, None),
            P(None, ("row", "col"), None, None),
            P(("row", "col"), None),
            P(None, ("row", "col")),
        ),
        out_specs=P(("row", "col"), None),
        check_vma=False,
    )
```

```python
import functools

import jax
import jax.numpy as jnp
from jax import lax
from jax.experimental import pallas as pl
from jax.experimental.pallas import tpu as pltpu
from jax.sharding import PartitionSpec as P

LEAF = 512
GROUPS = [[4], [4, 4, 4]]
SIZES = sum(GROUPS, [])
VMEM = pl.BlockSpec(memory_space=pltpu.VMEM)
ANY = pl.BlockSpec(memory_space=pl.ANY)


def swapped(block, axis, apart):
    count = lax.axis_size(axis)
    return lax.ppermute(block, axis, [(i, i ^ (1 << apart)) for i in range(count)])


def leaf_kernel(first, outs, moved, bases, *rest):
    held, arrived = rest[-2:]
    places = [(out, i) for out in rest[-2 - outs : -2] for i in range(out.shape[0])]
    copies = []
    for n in range(len(places)):
        copy = pltpu.make_async_copy(moved.at[pl.ds((first + n) * LEAF, LEAF)], held.at[n], arrived.at[n])
        copy.start()
        copies.append(copy)
    for n, (out, i) in enumerate(places):
        copies[n].wait()
        out[i] = jnp.dot(bases[first + n], held[n], preferred_element_type=jnp.float32).astype(jnp.bfloat16)


def mixed(maps, state, other):
    values = jnp.concatenate([state, other], axis=0)
    return jnp.dot(maps, values, preferred_element_type=jnp.float32).astype(jnp.bfloat16)


def level_kernel(level, first, maps, state, other, *rest):
    out = rest[-1]
    for i in range(state.shape[0]):
        out[i] = mixed(maps[level - 1, first + i], state[i], other[i])


def last_kernel(level, first, maps, state, other, expand, *rest):
    out, held, sent = rest[-3:]
    copies = []
    for i in range(state.shape[0]):
        g = first + i
        final = mixed(maps[level - 1, g], state[i], other[i])
        rows = expand[pl.ds(g * LEAF, LEAF), :]
        held[i] = jnp.dot(rows, final, preferred_element_type=jnp.float32).astype(jnp.bfloat16)
        copy = pltpu.make_async_copy(held.at[i], out.at[pl.ds(g * LEAF, LEAF)], sent.at[i])
        copy.start()
        copies.append(copy)
    for copy in copies:
        copy.wait()


def limit(mib):
    return pltpu.CompilerParams(vmem_limit_bytes=mib * 1024 * 1024)


def cost(flops, size):
    return pl.CostEstimate(flops=0, bytes_accessed=0, transcendentals=0)


def project(moved, bases, first, counts, after):
    rhs, rank_max = moved.shape[1], bases.shape[1]
    count = sum(counts)
    return pl.pallas_call(
        functools.partial(leaf_kernel, first, len(counts)),
        out_shape=[jax.ShapeDtypeStruct((n, rank_max, rhs), jnp.bfloat16) for n in counts],
        in_specs=[ANY, VMEM] + [ANY] * len(after),
        out_specs=[VMEM] * len(counts),
        scratch_shapes=[pltpu.VMEM((count, LEAF, rhs), jnp.bfloat16), pltpu.SemaphoreType.DMA((count,))],
        compiler_params=limit(24),
        cost_estimate=cost(2 * count * LEAF * rank_max * rhs, count * LEAF * rhs * 2),
        name="leaf",
    )(moved, bases, *after)


def advance(state, other, maps, level, first, after):
    count, rank_max, rhs = state.shape
    return pl.pallas_call(
        functools.partial(level_kernel, level, first),
        out_shape=jax.ShapeDtypeStruct(state.shape, jnp.bfloat16),
        in_specs=[VMEM] * 3 + [ANY] * len(after),
        out_specs=VMEM,
        compiler_params=limit(24),
        cost_estimate=cost(4 * count * rank_max * rank_max * rhs, count * rank_max * rhs * 2),
        name="level",
    )(maps, state, other, *after)


def finish(state, other, maps, expand, level, first, after):
    count, rank_max, rhs = state.shape
    return pl.pallas_call(
        functools.partial(last_kernel, level, first),
        out_shape=jax.ShapeDtypeStruct((expand.shape[0], rhs), jnp.bfloat16),
        in_specs=[VMEM] * 4 + [ANY] * len(after),
        out_specs=ANY,
        scratch_shapes=[pltpu.VMEM((count, LEAF, rhs), jnp.bfloat16), pltpu.SemaphoreType.DMA((count,))],
        input_output_aliases={4: 0} if first else {},
        compiler_params=limit(24),
        cost_estimate=cost(2 * count * rank_max * rhs * (LEAF + 2 * rank_max), count * LEAF * rhs * 2),
        name="finish",
    )(maps, state, other, expand, *after)


def on_device(points, leaf_bases, own_maps, partner_maps, expand_bases, ranks):
    moved = lax.all_to_all(points, ("row", "col"), split_axis=0, concat_axis=0, tiled=True)
    rank_max = leaf_bases.shape[1]
    keep = (jnp.arange(rank_max, dtype=jnp.int32) < ranks[:, :, None])[..., None]
    bases = jnp.where(keep[0], leaf_bases.reshape(-1, LEAF, rank_max).transpose(0, 2, 1), 0)
    maps = jnp.where(keep[1:], jnp.concatenate([own_maps, partner_maps], axis=3), 0)
    moved, bases, maps = lax.optimization_barrier((moved, bases, maps))
    col_bits = lax.axis_size("col").bit_length() - 1
    row_bits = lax.axis_size("row").bit_length() - 1
    pairs = [("col", col_bits - 1), ("col", col_bits - 2), ("col", col_bits - 3), ("row", row_bits - 1)]
    chunks, first = [], 0
    for count in SIZES:
        chunks.append((first, count))
        first += count
    states, last, first = [], [], 0
    for counts in GROUPS:
        states += project(moved, bases, first, counts, last)
        last = [states[-1]]
        first += sum(counts)
    for level in range(1, 4):
        others = [swapped(s, *pairs[level - 1]) for s in states]
        for c, (first, _) in enumerate(chunks):
            states[c] = advance(states[c], others[c], maps, level, first, last)
            last = [states[c]]
    others = [swapped(s, *pairs[3]) for s in states]
    last = []
    for (first, _), state, other in zip(chunks, states, others):
        last = [finish(state, other, maps, expand_bases, 4, first, last)]
    return last[0]


def solution(mesh):
    return jax.shard_map(
        on_device,
        mesh=mesh,
        in_specs=(
            P(("row", "col"), None),
            P(("row", "col"), None),
            P(None, ("row", "col"), None, None),
            P(None, ("row", "col"), None, None),
            P(("row", "col"), None),
            P(None, ("row", "col")),
        ),
        out_specs=P(("row", "col"), None),
        check_vma=False,
    )
```

```python
import functools

import jax
import jax.numpy as jnp
from jax import lax
from jax.experimental import pallas as pl
from jax.experimental.pallas import tpu as pltpu
from jax.sharding import PartitionSpec as P

LEAF = 512
LEAVES = [[4], [4, 4, 4]]
SPLITS = [[[4], [4], [4], [4]]]*3
VMEM = pl.BlockSpec(memory_space=pltpu.VMEM)
ANY = pl.BlockSpec(memory_space=pl.ANY)


def swapped(block, axis, apart):
    count = lax.axis_size(axis)
    return lax.ppermute(block, axis, [(i, i ^ (1 << apart)) for i in range(count)])


def leaf_kernel(first, outs, moved, bases, *rest):
    held, arrived = rest[-2:]
    places = [(out, i) for out in rest[-2 - outs : -2] for i in range(out.shape[0])]
    count = len(places)
    copy = pltpu.make_async_copy(moved.at[pl.ds(first * LEAF, count * LEAF)], held, arrived)
    copy.start()
    copy.wait()
    for n, (out, i) in enumerate(places):
        rows = held[pl.ds(n * LEAF, LEAF), :]
        out[i] = jnp.dot(bases[first + n], rows, preferred_element_type=jnp.float32).astype(jnp.bfloat16)


def mixed(maps, state, other):
    values = jnp.concatenate([state, other], axis=0)
    return jnp.dot(maps, values, preferred_element_type=jnp.float32).astype(jnp.bfloat16)


def level_kernel(level, first, outs, maps, state, other, *rest):
    places = [(out, i) for out in rest[-outs:] for i in range(out.shape[0])]
    for n, (out, i) in enumerate(places):
        out[i] = mixed(maps[level - 1, first + n], state[n], other[n])


def last_kernel(level, first, maps, state, other, expand, *rest):
    out, held, sent = rest[-3:]
    copies = []
    for i in range(state.shape[0]):
        g = first + i
        final = mixed(maps[level - 1, g], state[i], other[i])
        rows = expand[pl.ds(g * LEAF, LEAF), :]
        held[i] = jnp.dot(rows, final, preferred_element_type=jnp.float32).astype(jnp.bfloat16)
        copy = pltpu.make_async_copy(held.at[i], out.at[pl.ds(g * LEAF, LEAF)], sent.at[i])
        copy.start()
        copies.append(copy)
    for copy in copies:
        copy.wait()


def limit(mib):
    return pltpu.CompilerParams(vmem_limit_bytes=mib * 1024 * 1024)


def cost(flops, size):
    return pl.CostEstimate(flops=0, bytes_accessed=0, transcendentals=0)


def project(moved, bases, first, counts, after):
    rhs, rank_max = moved.shape[1], bases.shape[1]
    count = sum(counts)
    return pl.pallas_call(
        functools.partial(leaf_kernel, first, len(counts)),
        out_shape=[jax.ShapeDtypeStruct((n, rank_max, rhs), jnp.bfloat16) for n in counts],
        in_specs=[ANY, VMEM] + [ANY] * len(after),
        out_specs=[VMEM] * len(counts),
        scratch_shapes=[pltpu.VMEM((count * LEAF, rhs), jnp.bfloat16), pltpu.SemaphoreType.DMA],
        compiler_params=limit(24),
        cost_estimate=cost(2 * count * LEAF * rank_max * rhs, count * LEAF * rhs * 2),
        name="leaf",
    )(moved, bases, *after)


def advance(state, other, maps, level, first, counts, after):
    count, rank_max, rhs = state.shape
    return pl.pallas_call(
        functools.partial(level_kernel, level, first, len(counts)),
        out_shape=[jax.ShapeDtypeStruct((n, rank_max, rhs), jnp.bfloat16) for n in counts],
        in_specs=[VMEM] * 3 + [ANY] * len(after),
        out_specs=[VMEM] * len(counts),
        compiler_params=limit(24),
        cost_estimate=cost(4 * count * rank_max * rank_max * rhs, count * rank_max * rhs * 2),
        name="level",
    )(maps, state, other, *after)


def finish(state, other, maps, expand, level, first, after):
    count, rank_max, rhs = state.shape
    return pl.pallas_call(
        functools.partial(last_kernel, level, first),
        out_shape=jax.ShapeDtypeStruct((expand.shape[0], rhs), jnp.bfloat16),
        in_specs=[VMEM] * 4 + [ANY] * len(after),
        out_specs=ANY,
        scratch_shapes=[pltpu.VMEM((count, LEAF, rhs), jnp.bfloat16), pltpu.SemaphoreType.DMA((count,))],
        input_output_aliases={4: 0} if first else {},
        compiler_params=limit(24),
        cost_estimate=cost(2 * count * rank_max * rhs * (LEAF + 2 * rank_max), count * LEAF * rhs * 2),
        name="finish",
    )(maps, state, other, expand, *after)


def on_device(points, leaf_bases, own_maps, partner_maps, expand_bases, ranks):
    moved = lax.all_to_all(points, ("row", "col"), split_axis=0, concat_axis=0, tiled=True)
    rank_max = leaf_bases.shape[1]
    keep = (jnp.arange(rank_max, dtype=jnp.int32) < ranks[:, :, None])[..., None]
    bases = jnp.where(keep[0], leaf_bases.reshape(-1, LEAF, rank_max).transpose(0, 2, 1), 0)
    maps = jnp.where(keep[1:], jnp.concatenate([own_maps, partner_maps], axis=3), 0)
    moved, bases, maps = lax.optimization_barrier((moved, bases, maps))
    col_bits = lax.axis_size("col").bit_length() - 1
    row_bits = lax.axis_size("row").bit_length() - 1
    pairs = [("col", col_bits - 1), ("col", col_bits - 2), ("col", col_bits - 3), ("row", row_bits - 1)]
    states, last, first = [], [], 0
    for counts in LEAVES:
        states += project(moved, bases, first, counts, last)
        last = [states[-1]]
        first += sum(counts)
    for level in range(1, 4):
        others = [swapped(s, *pairs[level - 1]) for s in states]
        made, first = [], 0
        for counts, state, other in zip(SPLITS[level - 1], states, others):
            made += advance(state, other, maps, level, first, counts, last)
            last = [made[-1]]
            first += sum(counts)
        states = made
    others = [swapped(s, *pairs[3]) for s in states]
    last, first = [], 0
    for state, other in zip(states, others):
        last = [finish(state, other, maps, expand_bases, 4, first, last)]
        first += state.shape[0]
    return last[0]


def solution(mesh):
    return jax.shard_map(
        on_device,
        mesh=mesh,
        in_specs=(
            P(("row", "col"), None),
            P(("row", "col"), None),
            P(None, ("row", "col"), None, None),
            P(None, ("row", "col"), None, None),
            P(("row", "col"), None),
            P(None, ("row", "col")),
        ),
        out_specs=P(("row", "col"), None),
        check_vma=False,
    )
```
